32 devices in a mesh: layer: 8 (over z, core), feat: 4 (over y, x).
Axes of the slice: x: 2, y: 2, z: 4, core: 2. Of those that a mesh axis runs over, the one named last changes fastest.
Arguments:
- attn_heads: bfloat16 [8, 768, 2048], P('layer', None, 'feat'), may hold values from -6 to 6
- out_proj: bfloat16 [8, 2048, 2048], P('layer', 'feat'), may hold values from -0.125 to 0.125
- resid_pre: bfloat16 [8, 768, 2048], P('layer'), may hold values from -6 to 6
- enc_weight: bfloat16 [8, 2048, 16384], P('layer', None, 'feat'), may hold values from -0.03125 to 0.03125
- enc_bias: float32 [16384], P('feat'), may hold values from -4 to 4
- dec_weight: bfloat16 [8, 16384, 2048], P('layer', 'feat'), may hold values from -0.09375 to 0.09375
- dec_bias: float32 [8, 2048], P('layer', 'feat'), may hold values from -3 to 3
Outputs:
- features: float32 [768, 16384], P('layer', 'feat')
- rebuilt: float32 [8, 768, 2048], P('layer', None, 'feat')
The draws below stay inside these ranges and needn't reach their ends.
All inputs are finite; a program needn't handle non-finite values.
Results may differ from the reference program's by a relative error of at most 0.0035.
Values may be sent and summed in bfloat16 or wider, within the bound.
No kernel may reach another device: no remote copies, remote signals or barrier semaphores. Data moves between devices by JAX's collectives and lax.ppermute only.
A program may use at most 128 MiB of HBM per device.

```python
import jax
import jax.numpy as jnp

D = 2048
FEATS = 16384
TOKENS = 768
LAYERS = 8


def levels(rng, extent, pieces, low, largest):
    level, own = 1.0, jax.random.fold_in(rng, 6)
    for axis_at, parts in pieces:
        heights = jnp.exp(jax.random.uniform(jax.random.fold_in(own, axis_at), (parts,), jnp.float32, low / len(pieces), largest / len(pieces)))
        level = level * jnp.repeat(heights, extent[axis_at] // parts).reshape([-1 if axis == axis_at else 1 for axis in range(len(extent))])
    return level


def normal_values(own_key, extent, spread, bound, pieces=(), held_as=jnp.bfloat16):
    array = spread * jax.random.normal(own_key, extent, jnp.float32)
    if pieces:
        array = array * levels(own_key, extent, pieces, -0.22, 0.18)
    return jnp.clip(array, -bound, bound).astype(held_as)


def setup_inputs(seed: int = 0) -> dict:
    streams_of = jax.random.split(jax.random.key(seed), 8)
    return {
        "attn_heads": normal_values(streams_of[0], (LAYERS, TOKENS, D), 1.0, 6.0, ((0, 8), (2, 4))),
        "out_proj": normal_values(streams_of[1], (LAYERS, D, D), D ** -0.5, 0.125, ((0, 8), (1, 4))),
        "resid_pre": normal_values(streams_of[2], (LAYERS, TOKENS, D), 1.0, 6.0, ((0, 8),)),
        "enc_weight": normal_values(streams_of[3], (LAYERS, D, FEATS), (2 * D * LAYERS) ** -0.5, 0.03125, ((0, 8), (2, 4))),
        "enc_bias": normal_values(streams_of[4], (FEATS,), 0.7, 4.0, ((0, 4),), jnp.float32),
        "dec_weight": normal_values(streams_of[5], (LAYERS, FEATS, D), (FEATS // 4) ** -0.5, 0.09375, ((0, 8), (1, 4))),
        "dec_bias": normal_values(streams_of[6], (LAYERS, D), 0.5, 3.0, ((0, 8), (1, 4)), jnp.float32),
    }


def reference(attn_heads, out_proj, resid_pre, enc_weight, enc_bias, dec_weight, dec_bias):
    preact = jnp.zeros((TOKENS, FEATS), jnp.float32) + enc_bias[None, :]
    for layer in range(LAYERS):
        projected = jnp.dot(attn_heads[layer], out_proj[layer], preferred_element_type=jnp.float32)
        hidden_in = (resid_pre[layer].astype(jnp.float32) + projected).astype(jnp.bfloat16)
        preact = preact + jnp.dot(hidden_in, enc_weight[layer], preferred_element_type=jnp.float32)
    features = jnp.maximum(preact, 0.0)
    coded = features.astype(jnp.bfloat16)
    outputs = []
    for layer in range(LAYERS):
        outputs.append(dec_bias[layer][None, :] + jnp.dot(coded, dec_weight[layer], preferred_element_type=jnp.float32))
    return features, jnp.stack(outputs, axis=0)
```

```python
import functools

import jax
import jax.numpy as jnp
from jax import lax
from jax.experimental import pallas as pl
from jax.experimental.pallas import tpu as pltpu
from jax.sharding import PartitionSpec as P

F32 = jnp.float32
BF16 = jnp.bfloat16
VMEM_LIMIT = 6 * 2**20
UNIT = 16
PLANS = {
    6: (
        ((1,), (1,), (1, 1), (1, 1)),
        ((0, 1, 2), (3, 4), (5,)),
        (0, 3, 1, 0, 2, 0, 1, 0, 2, 1, 3, 4, 2, 4, 1, 3, 2, 4, 5, 3, 4, 5, 6, 4, 5, 6, 8, 5, 4, 6, 8, 7, 6, 7, 8, 5, 7, 6, 9, 8, 9, 7, 6, 5, 8, 10, 9, 7, 8, 9, 7, 10, 9, 11, 9, 12, 11, 10, 12, 11, 12),
    ),
}


def like(shape, dtype):
    return jax.ShapeDtypeStruct(shape, dtype)


class Core:
    def __init__(self, info):
        self.info = info
        self.last = info

    def run(self, name, body, out_shape, *args, far=0, scratch=(), flops=0):
        vmem = pl.BlockSpec(memory_space=pltpu.VMEM)
        args = lax.optimization_barrier((*args, self.last))[:-1]
        spaces = [pltpu.HBM] * far + [pltpu.VMEM] * (len(args) - far)

        moved = sum(a.size * a.dtype.itemsize for a in (*args, *out_shape))
        outs = pl.pallas_call(
            body,
            in_specs=[pl.BlockSpec(memory_space=pltpu.SMEM)]
            + [pl.BlockSpec(memory_space=space) for space in spaces],
            out_specs=[vmem] * len(out_shape),
            out_shape=list(out_shape),
            scratch_shapes=list(scratch),
            compiler_params=pltpu.CompilerParams(vmem_limit_bytes=VMEM_LIMIT),
            cost_estimate=pl.CostEstimate(flops=flops, bytes_accessed=moved, transcendentals=0),
            name=name,
        )(self.info, *map(pltpu.with_memory_space_constraint, args, spaces))
        self.last = min(outs, key=lambda a: a.size)
        return outs

    def fuse(self, function, *args):
        args = lax.optimization_barrier((*args, self.last))[:-1]
        self.last = function(*args)
        return self.last


def project(core, heads, residual, weight, off, r, span, F):
    K, D = weight.shape
    rows = span * r
    tile = min(1024, D)
    first = off == 0

    def body(info_ref, a_ref, res_ref, w_ref, keep, send, x, res, sems, *own):
        copies = [
            pltpu.make_async_copy(
                a_ref.at[pl.ds(info_ref[3 + m] * span, span), off : off + r],
                x.at[m * span : (m + 1) * span],
                sems.at[m],
            )
            for m in range(F)
        ]
        copies.append(
            pltpu.make_async_copy(
                res_ref.at[pl.ds(info_ref[3] * span, span), off : off + r], res, sems.at[F]
            )
        )
        if first:
            copies.append(pltpu.make_async_copy(w_ref, own[0], sems.at[F + 1]))
            w_ref = own[0]
        for copy in copies:
            copy.start()
        for copy in copies:
            copy.wait()

        @pl.loop(0, D // tile)
        def _(i):
            cols = pl.ds(pl.multiple_of(i * tile, tile), tile)
            acc = jnp.dot(x[...].reshape(F * rows, K), w_ref[:, cols], preferred_element_type=F32)
            for m in range(F):
                part = acc[m * rows : (m + 1) * rows]
                if m % 2:
                    send[m // 2, :, cols] = part.astype(send.dtype)
                elif m:
                    keep[m // 2, :, cols] = part
                else:
                    keep[0, :, cols] = part + res[:, :, cols].astype(F32).reshape(rows, tile)

    half = (F // 2, rows, D)
    return core.run(
        "project",
        body,
        [like(half, F32), like(half, BF16)],
        heads,
        residual,
        weight,
        far=3 if first else 2,
        scratch=[
            pltpu.VMEM((F * span, r, K), BF16),
            pltpu.VMEM((span, r, D), BF16),
            pltpu.SemaphoreType.DMA((F + 2,)),
        ]
        + [pltpu.VMEM((K, D), BF16)] * first,
        flops=2 * F * rows * K * D,
    )


def encode(core, near, far, weight, off, r, L, F):
    D, FL = weight.shape
    tile = min(1024, FL)
    span = L // F
    group = near.shape[1] // span

    def body(info_ref, near_ref, far_ref, w_ref, keep, send, x):
        me = info_ref[1]
        for m in range(F):
            for i in range(span):
                at = pl.multiple_of((info_ref[3 + m] * span + i) * r, r)
                rows = slice(i * group + off, i * group + off + r)
                x[pl.ds(at, r), :] = (far_ref if m % 2 else near_ref)[m // 2, rows, :]

        @pl.loop(0, FL // tile)
        def _(i):
            cols = pl.ds(pl.multiple_of(i * tile, tile), tile)
            acc = jnp.dot(x[...], w_ref[:, cols], preferred_element_type=F32)
            for p in range(L):
                m = me ^ p
                part = acc[p * r : (p + 1) * r]

                @pl.when(m % 2 == 0)
                def _():
                    keep[m // 2, :, cols] = part

                @pl.when(m % 2 == 1)
                def _():
                    send[m // 2, :, cols] = part.astype(send.dtype)

    half = (L // 2, r, FL)
    return core.run(
        "encode",
        body,
        [like(half, F32), like(half, BF16)],
        near,
        far,
        weight,
        scratch=[pltpu.VMEM((L * r, D), BF16)],
        flops=2 * L * r * D * FL,
    )


def decode(core, chunks, weight, L, F):
    FL, D = weight.shape
    wide = D // F
    sizes = [near.shape[1] for near, far in chunks]
    rows = L * sum(sizes)

    def body(info_ref, *refs):
        w_ref, keep, send, x = refs[2 * len(chunks) :]
        start = 0
        for c, r in enumerate(sizes):
            for m in range(L):
                at = pl.multiple_of(start + (info_ref[1] ^ m) * r, UNIT)
                x[pl.ds(at, r), :] = refs[2 * c + m % 2][m // 2]
            start += L * r

        @pl.loop(0, F // 2)
        def _(i):
            def product(m):
                cols = pl.ds(pl.multiple_of(info_ref[3 + m] * wide, wide), wide)
                return jnp.dot(x[...], w_ref[:, cols], preferred_element_type=F32)

            send[i] = product(2 * i + 1).astype(send.dtype)
            keep[i] = product(2 * i)

    half = (F // 2, rows, wide)
    return core.run(
        "decode",
        body,
        [like(half, F32), like(half, BF16)],
        *[a for pair in chunks for a in pair],
        weight,
        scratch=[pltpu.VMEM((rows, FL), BF16)],
        flops=2 * rows * D * FL,
    )


def total(parts):
    out = parts[0].astype(F32)
    for part in parts[1:]:
        out = out + part.astype(F32)
    return out


def reduce_steps(core, keep, send, exchange, stages, last_type=BF16):
    terms = [keep, exchange(send, 0)]
    yield
    for s in range(1, stages):
        sent_as = last_type if s == stages - 1 else BF16
        moved = core.fuse(lambda *ts: total([t[1::2] for t in ts]).astype(sent_as), *terms)
        terms = [t[0::2] for t in terms] + [exchange(moved, s)]
        yield
    return terms


def gather_steps(core, own, exchange, stages):
    near = own
    for s in range(stages - 1, 0, -1):
        far = exchange(near, s)
        yield
        shape = (2 * near.shape[0], *near.shape[1:])
        near = core.fuse(
            lambda a, b: jnp.stack([a, b], axis=1).reshape(shape), near, far
        )
    far = exchange(near, 0)
    yield
    return near, far


class Work:
    def __init__(self, core, L, F, arrays):
        self.core, self.L, self.F, self.arrays = core, L, F, arrays
        self.fbits, self.lbits = F.bit_length() - 1, L.bit_length() - 1
        self.hidden, self.coded, self.features, self.rebuilt = {}, {}, {}, {}

    def over_feat(self, a, s):
        pairs = []
        for l in range(self.L):
            bit = 1 << (self.fbits - 1 - s if l % 2 else s)
            pairs += [(l * self.F + i, l * self.F + (i ^ bit)) for i in range(self.F)]
        return lax.ppermute(a, ("layer", "feat"), pairs)

    def over_layer(self, a, s):
        return lax.ppermute(a, "layer", [(l, l ^ (1 << s)) for l in range(self.L)])

    def prepare(self, group, off, r, wide):
        core, span = self.core, self.L // self.F
        heads, residual, out_weight = self.arrays[:3]
        keep, send = project(core, heads, residual, out_weight, off, r, span, self.F)
        terms = yield from reduce_steps(core, keep, send, self.over_feat, self.fbits, wide)
        hidden = core.fuse(lambda *ts: total(ts).astype(BF16), *terms)
        self.hidden[group] = yield from gather_steps(core, hidden, self.over_feat, self.fbits)

    def activate(self, chunk, group, off, r):
        core = self.core
        encoder, enc_bias = self.arrays[3:5]
        keep, send = encode(core, *self.hidden[group], encoder, off, r, self.L, self.F)
        terms = yield from reduce_steps(core, keep, send, self.over_layer, self.lbits)
        feats = core.fuse(lambda *ts: jnp.maximum(total(ts) + enc_bias, 0.0), *terms)
        self.features[chunk] = feats[0]
        coded = feats.astype(BF16)
        self.coded[chunk] = yield from gather_steps(core, coded, self.over_layer, self.lbits)

    def rebuild(self, chunks, wide):
        core = self.core
        decoder, dec_bias = self.arrays[5:]
        pairs = [self.coded[c] for c in chunks]
        keep, send = decode(core, pairs, decoder, self.L, self.F)
        terms = yield from reduce_steps(core, keep, send, self.over_feat, self.fbits, wide)
        out = core.fuse(lambda *ts: total(ts) + dec_bias, *terms)[0]
        start = 0
        for c, (near, far) in zip(chunks, pairs):
            r = near.shape[1]
            self.rebuilt[c] = out[start : start + self.L * r].reshape(self.L, r, -1)
            start += self.L * r


def plan(units):
    if units in PLANS:
        return PLANS[units]
    groups = [(1,)] * units
    return groups, [(c,) for c in range(units)], []


def fast(L, Fn, heads, out_weight, residual, encoder, enc_bias, decoder, dec_bias):
    T, K = heads.shape
    D = out_weight.shape[1]
    per, span = T // L, L // Fn
    f = lax.axis_index("feat")
    layer = lax.axis_index("layer")
    fbits, lbits = Fn.bit_length() - 1, L.bit_length() - 1
    places = []
    for m in range(Fn):
        back = sum(1 << (fbits - 1 - s) for s in range(fbits) if m >> s & 1)
        places.append(f ^ jnp.where(layer % 2 == 0, m, back))
    core = Core(jnp.stack([f, layer, layer % 2, *places]).astype(jnp.int32))
    arrays = (
        heads.reshape(L, per, K),
        residual.reshape(L, per, D),
        out_weight,
        encoder,
        enc_bias[None, None],
        decoder,
        dec_bias[None, None],
    )
    work = Work(core, L, Fn, arrays)
    groups, joins, order = plan(per // UNIT)
    start = 0
    prepares, activates = [], []
    for g, sizes in enumerate(groups):
        prepares.append(work.prepare(g, start * UNIT, sum(sizes) * UNIT, F32 if g else BF16))
        off = 0
        for units in sizes:
            activates.append(work.activate(len(activates), g, off, units * UNIT))
            off += units * UNIT
        start += sum(sizes)
    rebuilds = [work.rebuild(j, BF16 if j == joins[-1] else F32) for j in joins]
    runs = prepares + activates + rebuilds
    left = [2 * work.fbits] * len(prepares) + [2 * work.lbits] * len(activates)
    left += [work.fbits + 1] * len(rebuilds)
    order = order or [c for c in range(len(runs)) for _ in range(left[c])]
    for c in order:
        next(runs[c], None)
        left[c] -= 1
        if left[c] == 0:
            next(runs[c], None)
    features = jnp.concatenate([work.features[c] for c in range(len(activates))], axis=0)
    rebuilt = jnp.concatenate([work.rebuilt[c] for c in range(len(activates))], axis=1)
    return features, rebuilt.reshape(1, T, -1)


def plain(heads, out_weight, residual, encoder, enc_bias, decoder, dec_bias):
    part = jnp.dot(heads, out_weight, preferred_element_type=F32)
    hidden = (residual.astype(F32) + lax.psum(part, "feat")).astype(BF16)
    pre = jnp.dot(hidden, encoder, preferred_element_type=F32)
    own = lax.psum_scatter(pre, "layer", scatter_dimension=0, tiled=True) + enc_bias[None, :]
    own = jnp.maximum(own, 0.0)
    coded = lax.all_gather(own.astype(BF16), "layer", axis=0, tiled=True)
    recon = jnp.dot(coded, decoder, preferred_element_type=F32)
    out = lax.psum_scatter(recon, "feat", scatter_dimension=1, tiled=True) + dec_bias[None, :]
    return own, out[None]


def per_device(L, Fn, attn_heads, out_proj, resid_pre, enc_weight, enc_bias, dec_weight, dec_bias):
    args = (attn_heads[0], out_proj[0], resid_pre[0], enc_weight[0], enc_bias, dec_weight[0], dec_bias[0])
    powers = L & (L - 1) == 0 and Fn & (Fn - 1) == 0
    if powers and Fn >= 2 and L >= 2 and L % Fn == 0 and args[0].shape[0] % (L * UNIT) == 0:
        return fast(L, Fn, *args)
    return plain(*args)


def solution(mesh):
    return jax.shard_map(
        functools.partial(per_device, mesh.shape["layer"], mesh.shape["feat"]),
        mesh=mesh,
        in_specs=(
            P("layer", None, "feat"),
            P("layer", "feat", None),
            P("layer", None, None),
            P("layer", None, "feat"),
            P("feat"),
            P("layer", "feat", None),
            P("layer", "feat"),
        ),
        out_specs=(P("layer", "feat"), P("layer", None, "feat")),
        check_vma=False,
    )
```

```python
import functools

import jax
import jax.numpy as jnp
from jax import lax
from jax.experimental import pallas as pl
from jax.experimental.pallas import tpu as pltpu
from jax.sharding import PartitionSpec as P

F32 = jnp.float32
BF16 = jnp.bfloat16
VMEM_LIMIT = 6 * 2**20
UNIT = 16
PLANS = {
    6: (
        ((1,), (1,), (1, 1), (1, 1)),
        ((0, 1, 2), (3, 4), (5,)),
        (0, 1, 0, 0, 1, 0, 2, 1, 3, 4, 1, 2, 4, 5, 4, 2, 5, 2, 4, 5, 6, 4, 3, 6, 5, 7, 4, 3, 6, 7, 3, 6, 5, 8, 7, 8, 7, 6, 9, 8, 5, 9, 7, 6, 8, 9, 10, 7, 8, 9, 10, 9, 8, 9, 11, 10, 12, 11, 12, 11, 12),
    ),
}


def like(shape, dtype):
    return jax.ShapeDtypeStruct(shape, dtype)


class Core:
    def __init__(self, info):
        self.info = info
        self.last = info

    def run(self, name, body, out_shape, *args, far=0, scratch=(), flops=0):
        vmem = pl.BlockSpec(memory_space=pltpu.VMEM)
        args = lax.optimization_barrier((*args, self.last))[:-1]
        spaces = [pltpu.HBM] * far + [pltpu.VMEM] * (len(args) - far)

        moved = sum(a.size * a.dtype.itemsize for a in (*args, *out_shape))
        outs = pl.pallas_call(
            body,
            in_specs=[pl.BlockSpec(memory_space=pltpu.SMEM)]
            + [pl.BlockSpec(memory_space=space) for space in spaces],
            out_specs=[vmem] * len(out_shape),
            out_shape=list(out_shape),
            scratch_shapes=list(scratch),
            compiler_params=pltpu.CompilerParams(vmem_limit_bytes=VMEM_LIMIT),
            cost_estimate=pl.CostEstimate(flops=flops, bytes_accessed=moved, transcendentals=0),
            name=name,
        )(self.info, *map(pltpu.with_memory_space_constraint, args, spaces))
        self.last = min(outs, key=lambda a: a.size)
        return outs

    def fuse(self, function, *args):
        args = lax.optimization_barrier((*args, self.last))[:-1]
        self.last = function(*args)
        return self.last


def project(core, heads, residual, weight, off, r, span, F):
    K, D = weight.shape
    rows = span * r
    tile = min(1024, D)
    first = off == 0

    def body(info_ref, res_ref, a_ref, w_ref, keep, send, x, res, sems, *own):
        fetch = pltpu.make_async_copy(
            res_ref.at[pl.ds(info_ref[3] * span, span), off : off + r], res, sems.at[F]
        )
        fetch.start()
        if first:
            copies = [
                pltpu.make_async_copy(
                    a_ref.at[pl.ds(info_ref[3 + m] * span, span), off : off + r],
                    x.at[m * span : (m + 1) * span],
                    sems.at[m],
                )
                for m in range(F)
            ]
            copies.append(pltpu.make_async_copy(w_ref, own[0], sems.at[F + 1]))
            w_ref = own[0]
            for copy in copies:
                copy.start()
            for copy in copies:
                copy.wait()
        else:
            for m in range(F):
                x[m * span : (m + 1) * span] = a_ref[pl.ds(info_ref[3 + m] * span, span), off : off + r, :]
        fetch.wait()

        @pl.loop(0, D // tile)
        def _(i):
            cols = pl.ds(pl.multiple_of(i * tile, tile), tile)
            acc = jnp.dot(x[...].reshape(F * rows, K), w_ref[:, cols], preferred_element_type=F32)
            for m in range(F):
                part = acc[m * rows : (m + 1) * rows]
                if m % 2:
                    send[m // 2, :, cols] = part.astype(send.dtype)
                elif m:
                    keep[m // 2, :, cols] = part
                else:
                    keep[0, :, cols] = part + res[:, :, cols].astype(F32).reshape(rows, tile)

    half = (F // 2, rows, D)
    return core.run(
        "project",
        body,
        [like(half, F32), like(half, BF16)],
        residual,
        heads,
        weight,
        far=3 if first else 1,
        scratch=[
            pltpu.VMEM((F * span, r, K), BF16),
            pltpu.VMEM((span, r, D), BF16),
            pltpu.SemaphoreType.DMA((F + 2,)),
        ]
        + [pltpu.VMEM((K, D), BF16)] * first,
        flops=2 * F * rows * K * D,
    )


def encode(core, near, far, weight, off, r, L, F):
    D, FL = weight.shape
    tile = min(1024, FL)
    span = L // F
    group = near.shape[1] // span

    def body(info_ref, near_ref, far_ref, w_ref, keep, send, x):
        me = info_ref[1]
        for m in range(F):
            for i in range(span):
                at = pl.multiple_of((info_ref[3 + m] * span + i) * r, r)
                rows = slice(i * group + off, i * group + off + r)
                x[pl.ds(at, r), :] = (far_ref if m % 2 else near_ref)[m // 2, rows, :]

        @pl.loop(0, FL // tile)
        def _(i):
            cols = pl.ds(pl.multiple_of(i * tile, tile), tile)
            acc = jnp.dot(x[...], w_ref[:, cols], preferred_element_type=F32)
            for p in range(L):
                m = me ^ p
                part = acc[p * r : (p + 1) * r]

                @pl.when(m % 2 == 0)
                def _():
                    keep[m // 2, :, cols] = part

                @pl.when(m % 2 == 1)
                def _():
                    send[m // 2, :, cols] = part.astype(send.dtype)

    half = (L // 2, r, FL)
    return core.run(
        "encode",
        body,
        [like(half, F32), like(half, BF16)],
        near,
        far,
        weight,
        scratch=[pltpu.VMEM((L * r, D), BF16)],
        flops=2 * L * r * D * FL,
    )


def decode(core, chunks, weight, L, F):
    FL, D = weight.shape
    wide = D // F
    sizes = [near.shape[1] for near, far in chunks]
    rows = L * sum(sizes)

    def body(info_ref, *refs):
        w_ref, keep, send, x = refs[2 * len(chunks) :]
        start = 0
        for c, r in enumerate(sizes):
            for m in range(L):
                at = pl.multiple_of(start + (info_ref[1] ^ m) * r, UNIT)
                x[pl.ds(at, r), :] = refs[2 * c + m % 2][m // 2]
            start += L * r

        @pl.loop(0, F // 2)
        def _(i):
            def product(m):
                cols = pl.ds(pl.multiple_of(info_ref[3 + m] * wide, wide), wide)
                return jnp.dot(x[...], w_ref[:, cols], preferred_element_type=F32)

            send[i] = product(2 * i + 1).astype(send.dtype)
            keep[i] = product(2 * i)

    half = (F // 2, rows, wide)
    return core.run(
        "decode",
        body,
        [like(half, F32), like(half, BF16)],
        *[a for pair in chunks for a in pair],
        weight,
        scratch=[pltpu.VMEM((rows, FL), BF16)],
        flops=2 * rows * D * FL,
    )


def total(parts):
    out = parts[0].astype(F32)
    for part in parts[1:]:
        out = out + part.astype(F32)
    return out


def reduce_steps(core, keep, send, exchange, stages, last_type=BF16):
    terms = [keep, exchange(send, 0)]
    yield
    for s in range(1, stages):
        sent_as = last_type if s == stages - 1 else BF16
        moved = core.fuse(lambda *ts: total([t[1::2] for t in ts]).astype(sent_as), *terms)
        terms = [t[0::2] for t in terms] + [exchange(moved, s)]
        yield
    return terms


def gather_steps(core, own, exchange, stages):
    near = own
    for s in range(stages - 1, 0, -1):
        far = exchange(near, s)
        yield
        shape = (2 * near.shape[0], *near.shape[1:])
        near = core.fuse(
            lambda a, b: jnp.stack([a, b], axis=1).reshape(shape), near, far
        )
    far = exchange(near, 0)
    yield
    return near, far


class Work:
    def __init__(self, core, L, F, arrays):
        self.core, self.L, self.F, self.arrays = core, L, F, arrays
        self.fbits, self.lbits = F.bit_length() - 1, L.bit_length() - 1
        self.hidden, self.coded, self.features, self.rebuilt = {}, {}, {}, {}

    def over_feat(self, a, s):
        pairs = []
        for l in range(self.L):
            bit = 1 << (self.fbits - 1 - s if l % 2 else s)
            pairs += [(l * self.F + i, l * self.F + (i ^ bit)) for i in range(self.F)]
        return lax.ppermute(a, ("layer", "feat"), pairs)

    def over_layer(self, a, s):
        return lax.ppermute(a, "layer", [(l, l ^ (1 << s)) for l in range(self.L)])

    def prepare(self, group, off, r, wide):
        core, span = self.core, self.L // self.F
        heads, residual, out_weight = self.arrays[:3]
        keep, send = project(core, heads, residual, out_weight, off, r, span, self.F)
        terms = yield from reduce_steps(core, keep, send, self.over_feat, self.fbits, wide)
        hidden = core.fuse(lambda *ts: total(ts).astype(BF16), *terms)
        self.hidden[group] = yield from gather_steps(core, hidden, self.over_feat, self.fbits)

    def activate(self, chunk, group, off, r):
        core = self.core
        encoder, enc_bias = self.arrays[3:5]
        keep, send = encode(core, *self.hidden[group], encoder, off, r, self.L, self.F)
        terms = yield from reduce_steps(core, keep, send, self.over_layer, self.lbits)
        feats = core.fuse(lambda *ts: jnp.maximum(total(ts) + enc_bias, 0.0), *terms)
        self.features[chunk] = feats[0]
        coded = feats.astype(BF16)
        self.coded[chunk] = yield from gather_steps(core, coded, self.over_layer, self.lbits)

    def rebuild(self, chunks, wide):
        core = self.core
        decoder, dec_bias = self.arrays[5:]
        pairs = [self.coded[c] for c in chunks]
        keep, send = decode(core, pairs, decoder, self.L, self.F)
        terms = yield from reduce_steps(core, keep, send, self.over_feat, self.fbits, wide)
        out = core.fuse(lambda *ts: total(ts) + dec_bias, *terms)[0]
        start = 0
        for c, (near, far) in zip(chunks, pairs):
            r = near.shape[1]
            self.rebuilt[c] = out[start : start + self.L * r].reshape(self.L, r, -1)
            start += self.L * r


def plan(units):
    if units in PLANS:
        return PLANS[units]
    groups = [(1,)] * units
    return groups, [(c,) for c in range(units)], []


def fast(L, Fn, heads, out_weight, residual, encoder, enc_bias, decoder, dec_bias):
    T, K = heads.shape
    D = out_weight.shape[1]
    per, span = T // L, L // Fn
    f = lax.axis_index("feat")
    layer = lax.axis_index("layer")
    fbits, lbits = Fn.bit_length() - 1, L.bit_length() - 1
    places = []
    for m in range(Fn):
        back = sum(1 << (fbits - 1 - s) for s in range(fbits) if m >> s & 1)
        places.append(f ^ jnp.where(layer % 2 == 0, m, back))
    core = Core(jnp.stack([f, layer, layer % 2, *places]).astype(jnp.int32))
    arrays = (
        heads.reshape(L, per, K),
        residual.reshape(L, per, D),
        out_weight,
        encoder,
        enc_bias[None, None],
        decoder,
        dec_bias[None, None],
    )
    work = Work(core, L, Fn, arrays)
    groups, joins, order = plan(per // UNIT)
    start = 0
    prepares, activates = [], []
    for g, sizes in enumerate(groups):
        prepares.append(work.prepare(g, start * UNIT, sum(sizes) * UNIT, F32 if g else BF16))
        off = 0
        for units in sizes:
            activates.append(work.activate(len(activates), g, off, units * UNIT))
            off += units * UNIT
        start += sum(sizes)
    rebuilds = [work.rebuild(j, BF16 if j == joins[-1] else F32) for j in joins]
    runs = prepares + activates + rebuilds
    left = [2 * work.fbits] * len(prepares) + [2 * work.lbits] * len(activates)
    left += [work.fbits + 1] * len(rebuilds)
    order = order or [c for c in range(len(runs)) for _ in range(left[c])]
    for c in order:
        next(runs[c], None)
        left[c] -= 1
        if left[c] == 0:
            next(runs[c], None)
    features = jnp.concatenate([work.features[c] for c in range(len(activates))], axis=0)
    rebuilt = jnp.concatenate([work.rebuilt[c] for c in range(len(activates))], axis=1)
    return features, rebuilt.reshape(1, T, -1)


def plain(heads, out_weight, residual, encoder, enc_bias, decoder, dec_bias):
    part = jnp.dot(heads, out_weight, preferred_element_type=F32)
    hidden = (residual.astype(F32) + lax.psum(part, "feat")).astype(BF16)
    pre = jnp.dot(hidden, encoder, preferred_element_type=F32)
    own = lax.psum_scatter(pre, "layer", scatter_dimension=0, tiled=True) + enc_bias[None, :]
    own = jnp.maximum(own, 0.0)
    coded = lax.all_gather(own.astype(BF16), "layer", axis=0, tiled=True)
    recon = jnp.dot(coded, decoder, preferred_element_type=F32)
    out = lax.psum_scatter(recon, "feat", scatter_dimension=1, tiled=True) + dec_bias[None, :]
    return own, out[None]


def per_device(L, Fn, attn_heads, out_proj, resid_pre, enc_weight, enc_bias, dec_weight, dec_bias):
    args = (attn_heads[0], out_proj[0], resid_pre[0], enc_weight[0], enc_bias, dec_weight[0], dec_bias[0])
    powers = L & (L - 1) == 0 and Fn & (Fn - 1) == 0
    if powers and Fn >= 2 and L >= 2 and L % Fn == 0 and args[0].shape[0] % (L * UNIT) == 0:
        return fast(L, Fn, *args)
    return plain(*args)


def solution(mesh):
    return jax.shard_map(
        functools.partial(per_device, mesh.shape["layer"], mesh.shape["feat"]),
        mesh=mesh,
        in_specs=(
            P("layer", None, "feat"),
            P("layer", "feat", None),
            P("layer", None, None),
            P("layer", None, "feat"),
            P("feat"),
            P("layer", "feat", None),
            P("layer", "feat"),
        ),
        out_specs=(P("layer", "feat"), P("layer", None, "feat")),
        check_vma=False,
    )
```
